32 devices in a mesh: head: 4 (over z), key: 8 (over y, x, core).
Axes of the slice: x: 2, y: 2, z: 4, core: 2. Of those that a mesh axis runs over, the one named last changes fastest.
Arguments:
- q_latent: bfloat16 [128, 256, 576], P('head'), may hold values from -48 to 48
- k_latent: bfloat16 [8192, 576], P('key'), may hold values from -6 to 6
- q_index: bfloat16 [256, 8192], P('head'), may hold values from -8 to 8
- k_index: bfloat16 [8192, 128], P('key'), may hold values from -6 to 6
- head_weight: float32 [256, 64], P('head'), may hold values from -4 to 4, as said below
- loss_weight: float32 [256], P('head'), may hold values from 2048 to 16384
- query_pos: int32 [256], replicated, may hold values from 0 to 8191, as said below
- key_start: int32 [256], replicated, may hold values from 0 to 8191, as said below
Outputs:
- grad_query: float32 [256, 8192], P('head', 'key')
- grad_key: float32 [8192, 128], P('key')
- grad_weight: float32 [256, 64], P('head', 'key')
The draws below stay inside these ranges and needn't reach their ends.
Inputs may be any that keep to these rules, and one draw needn't show every extreme that they name: `head_weight`: indexer head weights, of either sign. Query t sees the keys key_start[t] to query_pos[t]; some query sits at position 8191 and some at 0. key_start[t] <= query_pos[t] for every query t; some query starts at 0 and some at 8191.
All inputs are finite; a program needn't handle non-finite values.
Results may differ from the reference program's by a relative error of at most 0.0028.
Values sent between devices are 32-bit elements; how exact they have to be, the bound alone decides.
A program may use at most 128 MiB of HBM per device.

```python
import math
import jax
import jax.numpy as jnp
from jax import lax

H = 128
LAT = 576
QK_DIM = 192
IH = 64
ID = 128
Q_DEV = 64
QUERIES = 256
KEYS = 8192
N_HEAD = 4


def drawn_draw(subkey, out_shape, spread, limit):
    values = jax.random.normal(subkey, out_shape, jnp.float32) * spread
    return jnp.clip(values, -limit, limit)


def draw_everything(key):
    base_key = jax.random.fold_in(key, 7341)
    subkeys = jax.random.split(base_key, 9)
    shuffled = jax.random.permutation(subkeys[0], QUERIES)
    aligned = shuffled[:3]
    lowest_row = shuffled[3]
    last_row = shuffled[4]
    query_pos = jax.random.randint(subkeys[1], (QUERIES,), 0, KEYS).astype(jnp.int32)
    query_pos = query_pos.at[aligned].set(KEYS - 1)
    query_pos = query_pos.at[lowest_row].set(0)
    query_pos = query_pos.at[last_row].set(KEYS - 1)
    key_start = jax.random.randint(subkeys[2], (QUERIES,), 0, query_pos + 1).astype(jnp.int32)
    key_start = key_start.at[aligned].set(0)
    key_start = key_start.at[last_row].set(KEYS - 1)
    k_latent = drawn_draw(subkeys[4], (KEYS, LAT), 1.0, 6.0)
    q_latent = drawn_draw(subkeys[5], (H, QUERIES, LAT), 2.0, 12.0)
    k_index = drawn_draw(subkeys[6], (KEYS, ID), 1.0, 6.0)
    q_index = drawn_draw(subkeys[7], (QUERIES, IH, ID), 1.0, 6.0)
    head_weight = drawn_draw(subkeys[8], (QUERIES, IH), 0.7, 4.0)
    return (q_latent, k_latent, q_index.reshape(QUERIES, IH * ID), k_index, head_weight, query_pos, key_start)


def draw_q_latent(key, part):
    return draw_everything(key)[0].astype(jnp.bfloat16)


def draw_k_latent(key, part):
    return draw_everything(key)[1].astype(jnp.bfloat16)


def draw_q_index(key, part):
    return draw_everything(key)[2].astype(jnp.bfloat16)


def draw_k_index(key, part):
    return draw_everything(key)[3].astype(jnp.bfloat16)


def draw_head_weight(key, part):
    return draw_everything(key)[4]


def draw_query_pos(key, part):
    return draw_everything(key)[5]


def draw_key_start(key, part):
    return draw_everything(key)[6]


def level_of(own_key, extent, pieces, least, largest):
    loudness, own = 1.0, jax.random.fold_in(own_key, 6)
    for dim, blocks in pieces:
        heights = jnp.exp(jax.random.uniform(jax.random.fold_in(own, dim), (blocks,), jnp.float32, least / len(pieces), largest / len(pieces)))
        loudness = loudness * jnp.repeat(heights, extent[dim] // blocks).reshape([-1 if axis == dim else 1 for axis in range(len(extent))])
    return loudness


def setup_inputs(seed: int = 0) -> dict:
    key_of = jax.random.split(jax.random.key(seed), 9)
    q_latent = draw_q_latent(jax.random.fold_in(key_of[8], 71), 0)
    k_latent = draw_k_latent(jax.random.fold_in(key_of[8], 71), 0)
    q_index = draw_q_index(jax.random.fold_in(key_of[8], 71), 0)
    k_index = draw_k_index(jax.random.fold_in(key_of[8], 71), 0)
    head_weight = draw_head_weight(jax.random.fold_in(key_of[8], 71), 0)
    loss_weight = jnp.clip(jnp.exp(math.log(16384.0) - 2.0794415 * jax.random.uniform(key_of[5], (QUERIES,), jnp.float32) ** level_of(key_of[5], (QUERIES,), ((0, 4),), -0.2, 0.2)), 2048.0, 16384.0)
    query_pos = draw_query_pos(jax.random.fold_in(key_of[8], 71), 0)
    key_start = draw_key_start(jax.random.fold_in(key_of[8], 71), 0)
    return dict(q_latent=q_latent, k_latent=k_latent, q_index=q_index, k_index=k_index, head_weight=head_weight, loss_weight=loss_weight, query_pos=query_pos, key_start=key_start)


def reference(q_latent, k_latent, q_index, k_index, head_weight, loss_weight, query_pos, key_start):
    positions = jnp.arange(KEYS, dtype=jnp.int32)
    visible = (positions[None, :] >= key_start[:, None]) & (positions[None, :] <= query_pos[:, None])
    score_scale = 1.0 / math.sqrt(QK_DIM)

    def add_head(running, q_head):
        scores = jnp.dot(q_head, k_latent.T, preferred_element_type=jnp.float32) * score_scale
        masked = jnp.where(visible, scores, -jnp.inf)
        highest = lax.optimization_barrier(jnp.max(masked, axis=1, keepdims=True))
        exponents = jnp.where(visible, jnp.exp(scores - highest), 0.0)
        probabilities = exponents / lax.optimization_barrier(jnp.sum(exponents, axis=1, keepdims=True))
        return (running + probabilities, None)
    summed, _ = lax.scan(add_head, jnp.zeros((QUERIES, KEYS), jnp.float32), q_latent)
    target = summed / H
    index_scale = 1.0 / math.sqrt(ID)
    key_float = k_index.astype(jnp.float32)
    q_blocks = q_index.reshape(N_HEAD, Q_DEV, IH, ID)
    w_blocks = head_weight.reshape(N_HEAD, Q_DEV, IH)
    c_blocks = loss_weight.reshape(N_HEAD, Q_DEV)
    v_blocks = visible.reshape(N_HEAD, Q_DEV, KEYS)
    t_blocks = target.reshape(N_HEAD, Q_DEV, KEYS)

    def block_step(key_total, entries):
        q_block, w_block, c_block, seen_mask, t_block = entries
        q_float = q_block.astype(jnp.float32)
        head_dots = jnp.einsum('qjd,sd->qjs', q_float, key_float)
        rectified = jnp.maximum(head_dots, 0.0)
        index_scores = lax.optimization_barrier(jnp.sum(w_block[:, :, None] * rectified, axis=1)) * index_scale
        masked = jnp.where(seen_mask, index_scores, -jnp.inf)
        highest = lax.optimization_barrier(jnp.max(masked, axis=1, keepdims=True))
        exponents = jnp.where(seen_mask, jnp.exp(index_scores - highest), 0.0)
        index_probs = exponents / lax.optimization_barrier(jnp.sum(exponents, axis=1, keepdims=True))
        grad_scores = jnp.where(seen_mask, c_block[:, None] * (index_probs - t_block), 0.0)
        head_coef = w_block * index_scale
        head_grad = jnp.where(head_dots > 0.0, grad_scores[:, None, :] * head_coef[:, :, None], 0.0).astype(jnp.bfloat16)
        grad_float = head_grad.astype(jnp.float32)
        query_part = jnp.einsum('qjs,sd->qjd', grad_float, key_float)
        key_part = jnp.einsum('qjs,qjd->sd', grad_float, q_float)
        weight_part = lax.optimization_barrier(jnp.sum(grad_scores[:, None, :] * rectified, axis=2)) * index_scale
        return (key_total + key_part, (query_part, weight_part))
    grad_key, (query_parts, weight_parts) = lax.scan(block_step, jnp.zeros((KEYS, ID), jnp.float32), (q_blocks, w_blocks, c_blocks, v_blocks, t_blocks))
    grad_query = query_parts.reshape(QUERIES, IH * ID)
    grad_weight = weight_parts.reshape(QUERIES, IH)
    return (grad_query, grad_key, grad_weight)
```

```python
import functools
import math

import jax
import jax.numpy as jnp
from jax import lax
from jax.experimental import pallas as pl
from jax.experimental.pallas import tpu as pltpu
from jax.sharding import PartitionSpec as P

H = 128
QK_DIM = 192
LOW = -1e30
FLOOR = -1e29
LOG2E = math.log2(math.e)
NT = (((1,), (1,)), ((), ()))
VMEM_LIMIT = 56 * 1024 * 1024


def main_kernel(heads_step, q_ref, k_ref, start_ref, pos_ref, e_ref, high_ref, sum_ref, bias):
    step = pl.program_id(0)
    keys_here = k_ref.shape[0]
    factor = LOG2E / math.sqrt(QK_DIM)

    @pl.when(step == 0)
    def _():
        position = lax.broadcasted_iota(jnp.int32, bias.shape, 0) + lax.axis_index("key") * keys_here
        seen = (position >= start_ref[...]) & (position <= pos_ref[...])
        bias[...] = jnp.where(seen, 0.0, LOW)

    for i in range(heads_step):
        scores = lax.dot_general(k_ref[...], q_ref[i], NT, preferred_element_type=jnp.float32) + bias[...]
        high = jnp.maximum(jnp.max(scores, axis=0, keepdims=True), FLOOR)
        exponents = jnp.exp2((scores - high) * factor)
        e_ref[i] = exponents
        high_ref[pl.ds(step * heads_step + i, 1), :] = high
        sum_ref[pl.ds(step * heads_step + i, 1), :] = jnp.sum(exponents, axis=0, keepdims=True)


def target_kernel(e_ref, c_ref, out_ref):
    heads = e_ref.shape[0]
    total = e_ref[0] * c_ref[0:1, :]
    for h in range(1, heads):
        total = total + e_ref[h] * c_ref[h : h + 1, :]
    out_ref[...] = total.T


def stacked(q_ref, group, heads, dim):
    width = heads * dim
    block = q_ref[:, pl.ds(pl.multiple_of(group * width, width), width)]
    return jnp.concatenate([block[:, i * dim : (i + 1) * dim] for i in range(heads)], axis=0)


def index_kernel(q_ref, k_ref, w_ref, start_ref, pos_ref, scores_ref, high_ref, sum_ref):
    groups, rows, heads = w_ref.shape
    keys_here, dim = k_ref.shape
    scores_ref[...] = jnp.zeros_like(scores_ref)

    def lap(group, carry):
        dots = lax.dot_general(
            stacked(q_ref, group, heads, dim), k_ref[...], NT, preferred_element_type=jnp.float32
        )
        weights = w_ref[group]
        total = scores_ref[...]
        for i in range(heads):
            total = total + weights[:, i : i + 1] * jnp.maximum(dots[i * rows : (i + 1) * rows], 0.0)
        scores_ref[...] = total
        return carry

    lax.fori_loop(0, groups, lap, 0)
    position = lax.broadcasted_iota(jnp.int32, (rows, keys_here), 1) + lax.axis_index("key") * keys_here
    seen = (position >= start_ref[...]) & (position <= pos_ref[...])
    scores = jnp.where(seen, scores_ref[...] * (1.0 / math.sqrt(dim)), LOW)
    scores_ref[...] = scores
    high = jnp.maximum(jnp.max(scores, axis=1, keepdims=True), FLOOR)
    high_ref[...] = high
    sum_ref[...] = jnp.sum(jnp.exp(scores - high), axis=1, keepdims=True)


def grad_kernel(q_ref, k_ref, w_ref, scores_ref, target_ref, high_ref, sum_ref, loss_ref,
                query_ref, key_ref, weight_ref, key_t, grads):
    groups, rows, heads = w_ref.shape
    keys_here, dim = k_ref.shape
    scale = 1.0 / math.sqrt(dim)
    scores = scores_ref[...]
    probs = jnp.exp(scores - high_ref[...]) / sum_ref[...]
    grads[...] = jnp.where(
        scores > FLOOR, loss_ref[...] * (probs - target_ref[...] * (1.0 / H)), 0.0
    )
    key_t[...] = jnp.zeros_like(key_t)

    def lap(group, carry):
        queries = stacked(q_ref, group, heads, dim)
        dots = lax.dot_general(queries, k_ref[...], NT, preferred_element_type=jnp.float32)
        weights = w_ref[group] * scale
        pieces, sums = [], []
        for i in range(heads):
            own = dots[i * rows : (i + 1) * rows]
            g = grads[...]
            pieces.append(jnp.where(own > 0.0, g * weights[:, i : i + 1], 0.0).astype(jnp.bfloat16))
            sums.append(jnp.sum(g * jnp.maximum(own, 0.0), axis=1, keepdims=True))
        head_grad = jnp.concatenate(pieces, axis=0)
        part = jnp.dot(head_grad, k_ref[...], preferred_element_type=jnp.float32)
        query_ref[group] = jnp.concatenate(
            [part[i * rows : (i + 1) * rows] for i in range(heads)], axis=1
        )
        key_t[...] += jnp.dot(queries.T, head_grad, preferred_element_type=jnp.float32)
        weight_ref[group] = jnp.concatenate(sums, axis=1) * scale
        return carry

    lax.fori_loop(0, groups, lap, 0)
    key_ref[...] = key_t[...].T


def shards(q_latent, k_latent, q_index, k_index, head_weight, loss_weight, query_pos, key_start):
    heads_here, queries, lat = q_latent.shape
    keys_here = k_latent.shape[0]
    rows, index_width = q_index.shape
    index_heads = head_weight.shape[1]
    dim = k_index.shape[1]
    key_devices = lax.axis_size("key")
    group_heads = index_heads // key_devices
    factor = LOG2E / math.sqrt(QK_DIM)
    params = pltpu.CompilerParams(vmem_limit_bytes=VMEM_LIMIT)
    f32 = jnp.float32

    heads_step = 2
    whole = lambda *shape: pl.BlockSpec(shape, lambda *_: (0,) * len(shape))
    exponents, main_high, main_sum = pl.pallas_call(
        functools.partial(main_kernel, heads_step),
        grid=(heads_here // heads_step,),
        in_specs=[
            pl.BlockSpec((heads_step, queries, lat), lambda h: (h, 0, 0)),
            whole(keys_here, lat),
            whole(1, queries),
            whole(1, queries),
        ],
        out_specs=[
            pl.BlockSpec((heads_step, keys_here, queries), lambda h: (h, 0, 0)),
            whole(heads_here, queries),
            whole(heads_here, queries),
        ],
        out_shape=[
            jax.ShapeDtypeStruct((heads_here, keys_here, queries), f32),
            jax.ShapeDtypeStruct((heads_here, queries), f32),
            jax.ShapeDtypeStruct((heads_here, queries), f32),
        ],
        scratch_shapes=[pltpu.VMEM((keys_here, queries), f32)],
        compiler_params=params,
    )(q_latent, k_latent, key_start[None, :], query_pos[None, :])

    row_start = lax.axis_index("head") * rows
    own_pos = lax.dynamic_slice_in_dim(query_pos, row_start, rows)[:, None]
    own_start = lax.dynamic_slice_in_dim(key_start, row_start, rows)[:, None]
    weights = head_weight.reshape(rows, key_devices, group_heads).transpose(1, 0, 2)
    index_scores, index_high, index_sum = pl.pallas_call(
        index_kernel,
        out_shape=[
            jax.ShapeDtypeStruct((rows, keys_here), f32),
            jax.ShapeDtypeStruct((rows, 1), f32),
            jax.ShapeDtypeStruct((rows, 1), f32),
        ],
        compiler_params=params,
    )(q_index, k_index, weights, own_start, own_pos)

    stats = jnp.concatenate(
        [main_high.reshape(-1), main_sum.reshape(-1), index_high.reshape(-1), index_sum.reshape(-1)]
    )
    stats = lax.all_gather(stats, "key")
    size = heads_here * queries
    high_all = stats[:, :size]
    high = jnp.max(high_all, axis=0)
    total = jnp.sum(stats[:, size : 2 * size] * jnp.exp2((high_all - high) * factor), axis=0)
    coef = jnp.exp2((main_high.reshape(-1) - high) * factor) / total
    coef = coef.reshape(heads_here, queries)
    ihigh_all = stats[:, 2 * size : 2 * size + rows]
    ihigh = jnp.max(ihigh_all, axis=0)
    itotal = jnp.sum(stats[:, 2 * size + rows :] * jnp.exp(ihigh_all - ihigh), axis=0)

    tile = 128
    summed = pl.pallas_call(
        target_kernel,
        grid=(keys_here // tile,),
        in_specs=[
            pl.BlockSpec((heads_here, tile, queries), lambda s: (0, s, 0)),
            whole(heads_here, queries),
        ],
        out_specs=pl.BlockSpec((queries, tile), lambda s: (0, s)),
        out_shape=jax.ShapeDtypeStruct((queries, keys_here), f32),
        compiler_params=params,
    )(exponents, coef)
    target = lax.psum_scatter(summed, "head", scatter_dimension=0, tiled=True)

    query_part, key_part, weight_part = pl.pallas_call(
        grad_kernel,
        out_shape=[
            jax.ShapeDtypeStruct((key_devices, rows, index_width // key_devices), f32),
            jax.ShapeDtypeStruct((keys_here, dim), f32),
            jax.ShapeDtypeStruct((key_devices, rows, group_heads), f32),
        ],
        scratch_shapes=[pltpu.VMEM((dim, keys_here), f32), pltpu.VMEM((rows, keys_here), f32)],
        compiler_params=params,
    )(q_index, k_index, weights, index_scores, target, ihigh[:, None], itotal[:, None], loss_weight[:, None])

    grad_query = lax.psum_scatter(query_part, "key", scatter_dimension=0, tiled=False)
    grad_weight = lax.psum_scatter(weight_part, "key", scatter_dimension=0, tiled=False)
    grad_key = lax.psum(key_part, "head")
    return (grad_query, grad_key, grad_weight)


def solution(mesh):
    return jax.shard_map(
        shards,
        mesh=mesh,
        in_specs=(
            P("head", None, None),
            P("key", None),
            P("head", None),
            P("key", None),
            P("head", None),
            P("head"),
            P(),
            P(),
        ),
        out_specs=(P("head", "key"), P("key", None), P("head", "key")),
        check_vma=False,
    )
```

```python
import math

import jax
import jax.numpy as jnp
from jax import lax
from jax.experimental import pallas as pl
from jax.experimental.pallas import tpu as pltpu
from jax.sharding import PartitionSpec as P

H = 128
QK_DIM = 192
LOW = -1e30
FLOOR = -1e29
LOG2E = math.log2(math.e)
NT = (((1,), (1,)), ((), ()))
VMEM_LIMIT = 60 * 1024 * 1024


def stacked(q_ref, group, heads, dim):
    width = heads * dim
    block = q_ref[:, pl.ds(pl.multiple_of(group * width, width), width)]
    return jnp.concatenate([block[:, i * dim : (i + 1) * dim] for i in range(heads)], axis=0)


def kernel(q_hbm, k_ref, start_row, pos_row, qi_ref, ki_ref, w_ref, start_col, pos_col, loss_ref,
           gq_ref, gk_ref, gw_ref,
           e, bias, raw_a, raw_b, q_first, q_last, q_pair, stats, stats_in, coef,
           iscores, istats, istats_in, t_send, t_in, grads, key_t, key_sum, key_in,
           part_send, part_in,
           q_sem, st_send, st_recv, is_send, is_recv, tg_send, tg_recv, pt_send, pt_recv,
           kr_send, kr_recv, kg_send, kg_recv):
    heads = q_hbm.shape[0]
    keys_here, queries = bias.shape
    groups, rows, group_heads = w_ref.shape
    dim = ki_ref.shape[1]
    width = group_heads * dim
    key_devices, head_devices = lax.axis_size("key"), lax.axis_size("head")
    my_key, my_head = lax.axis_index("key"), lax.axis_index("head")
    factor = LOG2E / math.sqrt(QK_DIM)
    index_scale = 1.0 / math.sqrt(dim)
    first_key = my_key * keys_here
    f32 = jnp.float32

    def peer(axis, offset):
        return lax.rem(lax.axis_index(axis) + offset, lax.axis_size(axis))

    def send(src, dst, send_sem, recv_sem, axis, offset):
        return pltpu.make_async_remote_copy(
            src_ref=src, dst_ref=dst, send_sem=send_sem, recv_sem=recv_sem,
            device_id={axis: peer(axis, offset)}, device_id_type=pl.DeviceIdType.MESH)

    pairs = (heads - 2) // 2
    copy_first = pltpu.make_async_copy(q_hbm.at[0], q_first, q_sem.at[2])
    copy_last = pltpu.make_async_copy(q_hbm.at[heads - 1], q_last, q_sem.at[3])

    def copy_pair(i):
        slot = lax.rem(i, 2)
        return pltpu.make_async_copy(q_hbm.at[pl.ds(2 * i + 1, 2)], q_pair.at[slot], q_sem.at[slot])

    copy_first.start()
    copy_last.start()
    copy_pair(0).start()

    barrier = pltpu.get_barrier_semaphore()
    for axis, count in (("key", key_devices), ("head", head_devices)):
        for offset in range(1, count):
            pl.semaphore_signal(barrier, inc=1, device_id={axis: peer(axis, offset)},
                                device_id_type=pl.DeviceIdType.MESH)

    position = lax.broadcasted_iota(jnp.int32, bias.shape, 0) + first_key
    bias[...] = jnp.where((position >= start_row[...]) & (position <= pos_row[...]), 0.0, LOW)

    chunk = 256

    def stage(query, dst, src, src_high, src_head):
        high = jnp.full((1, queries), FLOOR, f32)
        total = jnp.zeros((1, queries), f32)
        for c in range(0, keys_here, chunk):
            if query is not None:
                scores = jnp.dot(k_ref[c : c + chunk], query[...], preferred_element_type=f32)
                scores = scores + bias[c : c + chunk]
                dst[c : c + chunk] = scores
                high = jnp.maximum(high, jnp.max(scores, axis=0, keepdims=True))
            if src is not None:
                exponents = jnp.exp2((src[c : c + chunk] - src_high) * factor)
                e[src_head, c : c + chunk] = exponents
                total = total + jnp.sum(exponents, axis=0, keepdims=True)
        if src is not None:
            stats[0, pl.ds(src_head, 1)] = src_high
            stats[1, pl.ds(src_head, 1)] = total
        return high

    copy_first.wait()
    high = stage(q_first, raw_a, None, None, None)

    def pair(i, high):
        copy_pair(i).wait()

        @pl.when(i + 1 < pairs)
        def _():
            copy_pair(i + 1).start()

        slot = lax.rem(i, 2)
        high = stage(q_pair.at[slot, 0], raw_b, raw_a, high, 2 * i)
        return stage(q_pair.at[slot, 1], raw_a, raw_b, high, 2 * i + 1)

    high = lax.fori_loop(0, pairs, pair, high)
    copy_last.wait()
    high = stage(q_last, raw_b, raw_a, high, heads - 2)
    stage(None, None, raw_b, high, heads - 1)

    pl.semaphore_wait(barrier, key_devices + head_devices - 2)

    def send_stats(d):
        return send(stats, stats_in.at[d - 1], st_send.at[d - 1], st_recv.at[d - 1], "key", d)

    for d in range(1, key_devices):
        send_stats(d).start()

    iscores[...] = jnp.zeros_like(iscores)

    def index_lap(group, carry):
        dots = lax.dot_general(stacked(qi_ref, group, group_heads, dim), ki_ref[...], NT,
                               preferred_element_type=f32)
        weights = w_ref[group]
        total = iscores[...]
        for i in range(group_heads):
            total = total + weights[:, i : i + 1] * jnp.maximum(dots[i * rows : (i + 1) * rows], 0.0)
        iscores[...] = total
        return carry

    lax.fori_loop(0, groups, index_lap, 0)
    position = lax.broadcasted_iota(jnp.int32, (rows, keys_here), 1) + first_key
    seen = (position >= start_col[...]) & (position <= pos_col[...])
    scores = jnp.where(seen, iscores[...] * index_scale, LOW)
    iscores[...] = scores
    high = jnp.maximum(jnp.max(scores, axis=1, keepdims=True), FLOOR)
    total = jnp.sum(jnp.exp(scores - high), axis=1, keepdims=True)
    lane = lax.broadcasted_iota(jnp.int32, istats.shape, 1)
    istats[...] = jnp.where(lane == 0, high, jnp.where(lane == 1, total, 0.0))

    def send_istats(d):
        return send(istats, istats_in.at[d - 1], is_send.at[d - 1], is_recv.at[d - 1], "key", d)

    for d in range(1, key_devices):
        send_istats(d).start()

    for d in range(1, key_devices):
        send_stats(d).wait()
    high = stats[0]
    for d in range(1, key_devices):
        high = jnp.maximum(high, stats_in[d - 1, 0])
    own = jnp.exp2((stats[0] - high) * factor)
    total = stats[1] * own
    for d in range(1, key_devices):
        total = total + stats_in[d - 1, 1] * jnp.exp2((stats_in[d - 1, 0] - high) * factor)
    coef[...] = own / total

    tile = 128
    halves = t_send.shape[0]
    half = keys_here // halves

    def send_target(d, part):
        return send(t_send.at[part, peer("head", d)], t_in.at[d - 1, part],
                    tg_send.at[d - 1, part], tg_recv.at[d - 1, part], "head", d)

    for part in range(halves):
        for c in range(0, half, tile):
            at = part * half + c
            total = e[0, at : at + tile] * coef[0:1]
            for h in range(1, heads):
                total = total + e[h, at : at + tile] * coef[h : h + 1]
            across = total.T
            for z in range(head_devices):
                t_send[part, z, :, c : c + tile] = across[z * rows : (z + 1) * rows]
        for d in range(1, head_devices):
            send_target(d, part).start()

    for d in range(1, key_devices):
        send_istats(d).wait()
    high = istats[:, 0:1]
    for d in range(1, key_devices):
        high = jnp.maximum(high, istats_in[d - 1, :, 0:1])
    total = istats[:, 1:2] * jnp.exp(istats[:, 0:1] - high)
    for d in range(1, key_devices):
        total = total + istats_in[d - 1, :, 1:2] * jnp.exp(istats_in[d - 1, :, 0:1] - high)
    scores = iscores[...]
    iscores[...] = jnp.exp(scores - high) / total

    for part in range(halves):
        for d in range(1, head_devices):
            send_target(d, part).wait()
        span = slice(part * half, (part + 1) * half)
        target = t_send[part, my_head]
        for d in range(1, head_devices):
            target = target + t_in[d - 1, part]
        grads[:, span] = jnp.where(
            seen[:, span], loss_ref[...] * (iscores[:, span] - target * (1.0 / H)), 0.0)

    key_t[...] = jnp.zeros_like(key_t)

    def send_part(d):
        return send(part_send.at[d], part_in.at[d - 1], pt_send.at[d - 1], pt_recv.at[d - 1], "key", d)

    def grad_lap(lap, carry):
        d = key_devices - 1 - lap
        group = peer("key", d)
        stack = stacked(qi_ref, group, group_heads, dim)
        dots = lax.dot_general(stack, ki_ref[...], NT, preferred_element_type=f32)
        weights = w_ref[group] * index_scale
        pieces, sums = [], []
        for i in range(group_heads):
            own = dots[i * rows : (i + 1) * rows]
            g = grads[...]
            pieces.append(jnp.where(own > 0.0, g * weights[:, i : i + 1], 0.0).astype(jnp.bfloat16))
            sums.append(jnp.sum(g * jnp.maximum(own, 0.0), axis=1, keepdims=True))
        head_grad = jnp.concatenate(pieces, axis=0)
        part = jnp.dot(head_grad, ki_ref[...], preferred_element_type=f32)
        for i in range(group_heads):
            part_send[d, :, i * dim : (i + 1) * dim] = part[i * rows : (i + 1) * rows]
        lane = lax.broadcasted_iota(jnp.int32, (rows, 128), 1)
        extra = jnp.zeros((rows, 128), f32)
        for i in range(group_heads):
            extra = jnp.where(lane == i, sums[i], extra)
        part_send[d, :, width:] = extra * index_scale

        @pl.when(d > 0)
        def _():
            send_part(d).start()

        key_t[...] += jnp.dot(stack.T, head_grad, preferred_element_type=f32)
        return carry

    lax.fori_loop(0, key_devices, grad_lap, 0)

    block = keys_here // head_devices
    key_sum[...] = key_t[...].T.reshape(head_devices, block, dim)

    def reduce_key(d):
        return send(key_sum.at[peer("head", d)], key_in.at[d - 1],
                    kr_send.at[d - 1], kr_recv.at[d - 1], "head", d)

    def gather_key(d):
        return send(gk_ref.at[my_head], gk_ref.at[my_head],
                    kg_send.at[d - 1], kg_recv.at[d - 1], "head", d)

    for d in range(1, head_devices):
        reduce_key(d).start()
    for d in range(1, head_devices):
        reduce_key(d).wait()
    total = key_sum[my_head]
    for d in range(1, head_devices):
        total = total + key_in[d - 1]
    gk_ref[my_head] = total
    for d in range(1, head_devices):
        gather_key(d).start()

    gq_ref[...] = part_send[0, :, :width]
    gw_ref[...] = part_send[0, :, width : width + group_heads]
    for d in range(1, key_devices):
        send_part(d).wait()
        gq_ref[...] += part_in[d - 1, :, :width]
        gw_ref[...] += part_in[d - 1, :, width : width + group_heads]
    for d in range(1, head_devices):
        gather_key(d).wait()


def shards(q_latent, k_latent, q_index, k_index, head_weight, loss_weight, query_pos, key_start):
    heads_here, queries, lat = q_latent.shape
    keys_here = k_latent.shape[0]
    rows, index_width = q_index.shape
    index_heads = head_weight.shape[1]
    dim = k_index.shape[1]
    nk, nh = lax.axis_size("key"), lax.axis_size("head")
    group_heads = index_heads // nk
    width = index_width // nk
    f32, bf16 = jnp.float32, jnp.bfloat16
    row_start = lax.axis_index("head") * rows
    own_pos = lax.dynamic_slice_in_dim(query_pos, row_start, rows)[:, None]
    own_start = lax.dynamic_slice_in_dim(key_start, row_start, rows)[:, None]
    weights = head_weight.reshape(rows, nk, group_heads).transpose(1, 0, 2)
    halves = 2
    dma = lambda *shape: pltpu.SemaphoreType.DMA(shape)
    in_vmem = pl.BlockSpec(memory_space=pltpu.VMEM)
    grad_query, grad_key, grad_weight = pl.pallas_call(
        kernel,
        in_specs=[pl.BlockSpec(memory_space=pl.ANY)] + [in_vmem] * 9,
        out_specs=[in_vmem] * 3,
        out_shape=[
            jax.ShapeDtypeStruct((rows, width), f32),
            jax.ShapeDtypeStruct((nh, keys_here // nh, dim), f32),
            jax.ShapeDtypeStruct((rows, group_heads), f32),
        ],
        scratch_shapes=[
            pltpu.VMEM((heads_here, keys_here, queries), f32),
            pltpu.VMEM((keys_here, queries), f32),
            pltpu.VMEM((keys_here, queries), f32),
            pltpu.VMEM((keys_here, queries), f32),
            pltpu.VMEM((lat, queries), bf16),
            pltpu.VMEM((lat, queries), bf16),
            pltpu.VMEM((2, 2, lat, queries), bf16),
            pltpu.VMEM((2, heads_here, queries), f32),
            pltpu.VMEM((nk - 1, 2, heads_here, queries), f32),
            pltpu.VMEM((heads_here, queries), f32),
            pltpu.VMEM((rows, keys_here), f32),
            pltpu.VMEM((rows, 128), f32),
            pltpu.VMEM((nk - 1, rows, 128), f32),
            pltpu.VMEM((halves, nh, rows, keys_here // halves), f32),
            pltpu.VMEM((nh - 1, halves, rows, keys_here // halves), f32),
            pltpu.VMEM((rows, keys_here), f32),
            pltpu.VMEM((dim, keys_here), f32),
            pltpu.VMEM((nh, keys_here // nh, dim), f32),
            pltpu.VMEM((nh - 1, keys_here // nh, dim), f32),
            pltpu.VMEM((nk, rows, width + 128), f32),
            pltpu.VMEM((nk - 1, rows, width + 128), f32),
            dma(4),
            dma(nk - 1), dma(nk - 1), dma(nk - 1), dma(nk - 1),
            dma(nh - 1, halves), dma(nh - 1, halves),
            dma(nk - 1), dma(nk - 1),
            dma(nh - 1), dma(nh - 1), dma(nh - 1), dma(nh - 1),
        ],
        compiler_params=pltpu.CompilerParams(
            collective_id=0, has_side_effects=True, vmem_limit_bytes=VMEM_LIMIT),
    )(q_latent.transpose(0, 2, 1), k_latent, key_start[None, :], query_pos[None, :], q_index, k_index,
      weights, own_start, own_pos, loss_weight[:, None])
    return (grad_query, grad_key.reshape(keys_here, dim), grad_weight)


def solution(mesh):
    return jax.shard_map(
        shards,
        mesh=mesh,
        in_specs=(
            P("head", None, None),
            P("key", None),
            P("head", None),
            P("key", None),
            P("head", None),
            P("head"),
            P(),
            P(),
        ),
        out_specs=(P("head", "key"), P("key", None), P("head", "key")),
        check_vma=False,
    )
```

```python
import math

import jax
import jax.numpy as jnp
from jax import lax
from jax.experimental import pallas as pl
from jax.experimental.pallas import tpu as pltpu
from jax.sharding import PartitionSpec as P

H = 128
QK_DIM = 192
LOW = -1e30
FLOOR = -1e29
LOG2E = math.log2(math.e)
NT = (((1,), (1,)), ((), ()))
VMEM_LIMIT = 60 * 1024 * 1024


def stacked(q_ref, group, heads, dim):
    width = heads * dim
    block = q_ref[:, pl.ds(pl.multiple_of(group * width, width), width)]
    return jnp.concatenate([block[:, i * dim : (i + 1) * dim] for i in range(heads)], axis=0)


def column(row, first, rows):
    shape = (rows, row.shape[1])
    down, across = (lax.broadcasted_iota(jnp.int32, shape, i) for i in (0, 1))
    return jnp.sum(jnp.where(across == down + first, row, 0.0), axis=1, keepdims=True)


def kernel(q_hbm, kt_ref, start_row, pos_row, qi_ref, ki_ref, weight_ref, loss_row,
           gq_ref, gk_ref, gw_ref,
           k_ref, w_ref, e, bias, raw_a, raw_b, q_first, q_last, q_pair, stats, stats_in, coef,
           iscores, istats, istats_in, t_send, t_in, grads, key_t, key_sum, key_in,
           part_send, part_in,
           q_sem, st_send, st_recv, is_send, is_recv, tg_send, tg_recv, pt_send, pt_recv,
           kr_send, kr_recv, kg_send, kg_recv):
    heads = q_hbm.shape[0]
    keys_here, queries = bias.shape
    groups, rows, group_heads = w_ref.shape
    dim = ki_ref.shape[1]
    width = group_heads * dim
    key_devices, head_devices = lax.axis_size("key"), lax.axis_size("head")
    my_key, my_head = lax.axis_index("key"), lax.axis_index("head")
    factor = LOG2E / math.sqrt(QK_DIM)
    index_scale = 1.0 / math.sqrt(dim)
    first_key = my_key * keys_here
    f32 = jnp.float32

    def peer(axis, offset):
        return lax.rem(lax.axis_index(axis) + offset, lax.axis_size(axis))

    def send(src, dst, send_sem, recv_sem, axis, offset):
        return pltpu.make_async_remote_copy(
            src_ref=src, dst_ref=dst, send_sem=send_sem, recv_sem=recv_sem,
            device_id={axis: peer(axis, offset)}, device_id_type=pl.DeviceIdType.MESH)

    pairs = (heads - 2) // 2
    copy_first = pltpu.make_async_copy(q_hbm.at[0], q_first, q_sem.at[2])
    copy_last = pltpu.make_async_copy(q_hbm.at[heads - 1], q_last, q_sem.at[3])

    def copy_pair(i):
        slot = lax.rem(i, 2)
        return pltpu.make_async_copy(q_hbm.at[pl.ds(2 * i + 1, 2)], q_pair.at[slot], q_sem.at[slot])

    copy_first.start()
    copy_last.start()
    copy_pair(0).start()

    barrier = pltpu.get_barrier_semaphore()
    for axis, count in (("key", key_devices), ("head", head_devices)):
        for offset in range(1, count):
            pl.semaphore_signal(barrier, inc=1, device_id={axis: peer(axis, offset)},
                                device_id_type=pl.DeviceIdType.MESH)

    k_ref[...] = kt_ref[...].T
    for g in range(groups):
        w_ref[g] = weight_ref[:, g * group_heads : (g + 1) * group_heads]
    position = lax.broadcasted_iota(jnp.int32, bias.shape, 0) + first_key
    bias[...] = jnp.where((position >= start_row[...]) & (position <= pos_row[...]), 0.0, LOW)

    chunk = 256

    def stage(query, dst, src, src_high, src_head):
        high = jnp.full((1, queries), FLOOR, f32)
        total = jnp.zeros((1, queries), f32)
        for c in range(0, keys_here, chunk):
            if query is not None:
                scores = jnp.dot(k_ref[c : c + chunk], query[...], preferred_element_type=f32)
                scores = scores + bias[c : c + chunk]
                dst[c : c + chunk] = scores
                high = jnp.maximum(high, jnp.max(scores, axis=0, keepdims=True))
            if src is not None:
                exponents = jnp.exp2((src[c : c + chunk] - src_high) * factor)
                e[src_head, c : c + chunk] = exponents
                total = total + jnp.sum(exponents, axis=0, keepdims=True)
        if src is not None:
            stats[0, pl.ds(src_head, 1)] = src_high
            stats[1, pl.ds(src_head, 1)] = total
        return high

    copy_first.wait()
    high = stage(q_first, raw_a, None, None, None)

    def pair(i, high):
        copy_pair(i).wait()

        @pl.when(i + 1 < pairs)
        def _():
            copy_pair(i + 1).start()

        slot = lax.rem(i, 2)
        high = stage(q_pair.at[slot, 0], raw_b, raw_a, high, 2 * i)
        return stage(q_pair.at[slot, 1], raw_a, raw_b, high, 2 * i + 1)

    high = lax.fori_loop(0, pairs, pair, high)
    copy_last.wait()
    high = stage(q_last, raw_b, raw_a, high, heads - 2)
    stage(None, None, raw_b, high, heads - 1)

    pl.semaphore_wait(barrier, key_devices + head_devices - 2)

    def send_stats(d):
        return send(stats, stats_in.at[d - 1], st_send.at[d - 1], st_recv.at[d - 1], "key", d)

    for d in range(1, key_devices):
        send_stats(d).start()

    iscores[...] = jnp.zeros_like(iscores)

    def index_lap(group, carry):
        dots = lax.dot_general(stacked(qi_ref, group, group_heads, dim), ki_ref[...], NT,
                               preferred_element_type=f32)
        weights = w_ref[group]
        total = iscores[...]
        for i in range(group_heads):
            total = total + weights[:, i : i + 1] * jnp.maximum(dots[i * rows : (i + 1) * rows], 0.0)
        iscores[...] = total
        return carry

    lax.fori_loop(0, groups, index_lap, 0)
    position = lax.broadcasted_iota(jnp.int32, (rows, keys_here), 1) + first_key
    own_start = column(start_row[...].astype(f32), my_head * rows, rows)
    own_pos = column(pos_row[...].astype(f32), my_head * rows, rows)
    loss = column(loss_row[...], 0, rows)
    position = position.astype(f32)
    seen = (position >= own_start) & (position <= own_pos)
    scores = jnp.where(seen, iscores[...] * index_scale, LOW)
    iscores[...] = scores
    high = jnp.maximum(jnp.max(scores, axis=1, keepdims=True), FLOOR)
    total = jnp.sum(jnp.exp(scores - high), axis=1, keepdims=True)
    lane = lax.broadcasted_iota(jnp.int32, istats.shape, 1)
    istats[...] = jnp.where(lane == 0, high, jnp.where(lane == 1, total, 0.0))

    def send_istats(d):
        return send(istats, istats_in.at[d - 1], is_send.at[d - 1], is_recv.at[d - 1], "key", d)

    for d in range(1, key_devices):
        send_istats(d).start()

    for d in range(1, key_devices):
        send_stats(d).wait()
    high = stats[0]
    for d in range(1, key_devices):
        high = jnp.maximum(high, stats_in[d - 1, 0])
    own = jnp.exp2((stats[0] - high) * factor)
    total = stats[1] * own
    for d in range(1, key_devices):
        total = total + stats_in[d - 1, 1] * jnp.exp2((stats_in[d - 1, 0] - high) * factor)
    coef[...] = own / total

    tile = 128
    halves = t_send.shape[0]
    half = keys_here // halves

    def send_target(d, part):
        return send(t_send.at[part, peer("head", d)], t_in.at[d - 1, part],
                    tg_send.at[d - 1, part], tg_recv.at[d - 1, part], "head", d)

    for part in range(halves):
        for c in range(0, half, tile):
            at = part * half + c
            total = e[0, at : at + tile] * coef[0:1]
            for h in range(1, heads):
                total = total + e[h, at : at + tile] * coef[h : h + 1]
            across = total.T
            for z in range(head_devices):
                t_send[part, z, :, c : c + tile] = across[z * rows : (z + 1) * rows]
        for d in range(1, head_devices):
            send_target(d, part).start()

    for d in range(1, key_devices):
        send_istats(d).wait()
    high = istats[:, 0:1]
    for d in range(1, key_devices):
        high = jnp.maximum(high, istats_in[d - 1, :, 0:1])
    total = istats[:, 1:2] * jnp.exp(istats[:, 0:1] - high)
    for d in range(1, key_devices):
        total = total + istats_in[d - 1, :, 1:2] * jnp.exp(istats_in[d - 1, :, 0:1] - high)
    scores = iscores[...]
    iscores[...] = jnp.exp(scores - high) / total

    for part in range(halves):
        for d in range(1, head_devices):
            send_target(d, part).wait()
        span = slice(part * half, (part + 1) * half)
        target = t_send[part, my_head]
        for d in range(1, head_devices):
            target = target + t_in[d - 1, part]
        grads[:, span] = jnp.where(
            seen[:, span], loss * (iscores[:, span] - target * (1.0 / H)), 0.0)

    key_t[...] = jnp.zeros_like(key_t)

    def send_part(d):
        return send(part_send.at[d], part_in.at[d - 1], pt_send.at[d - 1], pt_recv.at[d - 1], "key", d)

    def grad_lap(lap, carry):
        d = key_devices - 1 - lap
        group = peer("key", d)
        stack = stacked(qi_ref, group, group_heads, dim)
        dots = lax.dot_general(stack, ki_ref[...], NT, preferred_element_type=f32)
        weights = w_ref[group] * index_scale
        pieces, sums = [], []
        for i in range(group_heads):
            own = dots[i * rows : (i + 1) * rows]
            g = grads[...]
            pieces.append(jnp.where(own > 0.0, g * weights[:, i : i + 1], 0.0).astype(jnp.bfloat16))
            sums.append(jnp.sum(g * jnp.maximum(own, 0.0), axis=1, keepdims=True))
        head_grad = jnp.concatenate(pieces, axis=0)
        part = jnp.dot(head_grad, ki_ref[...], preferred_element_type=f32)
        for i in range(group_heads):
            part_send[d, :, i * dim : (i + 1) * dim] = part[i * rows : (i + 1) * rows]
        lane = lax.broadcasted_iota(jnp.int32, (rows, 128), 1)
        extra = jnp.zeros((rows, 128), f32)
        for i in range(group_heads):
            extra = jnp.where(lane == i, sums[i], extra)
        part_send[d, :, width:] = extra * index_scale

        @pl.when(d > 0)
        def _():
            send_part(d).start()

        key_t[...] += jnp.dot(stack.T, head_grad, preferred_element_type=f32)
        return carry

    lax.fori_loop(0, key_devices, grad_lap, 0)

    block = keys_here // head_devices
    key_sum[...] = key_t[...].T.reshape(head_devices, block, dim)

    def reduce_key(d):
        return send(key_sum.at[peer("head", d)], key_in.at[d - 1],
                    kr_send.at[d - 1], kr_recv.at[d - 1], "head", d)

    def gather_key(d):
        return send(gk_ref.at[my_head], gk_ref.at[my_head],
                    kg_send.at[d - 1], kg_recv.at[d - 1], "head", d)

    for d in range(1, head_devices):
        reduce_key(d).start()
    for d in range(1, head_devices):
        reduce_key(d).wait()
    total = key_sum[my_head]
    for d in range(1, head_devices):
        total = total + key_in[d - 1]
    gk_ref[my_head] = total
    for d in range(1, head_devices):
        gather_key(d).start()

    gq_ref[...] = part_send[0, :, :width]
    gw_ref[...] = part_send[0, :, width : width + group_heads]
    for d in range(1, key_devices):
        send_part(d).wait()
        gq_ref[...] += part_in[d - 1, :, :width]
        gw_ref[...] += part_in[d - 1, :, width : width + group_heads]
    for d in range(1, head_devices):
        gather_key(d).wait()


def shards(q_latent, k_latent, q_index, k_index, head_weight, loss_weight, query_pos, key_start):
    heads_here, queries, lat = q_latent.shape
    keys_here = k_latent.shape[0]
    rows, index_width = q_index.shape
    index_heads = head_weight.shape[1]
    dim = k_index.shape[1]
    nk, nh = lax.axis_size("key"), lax.axis_size("head")
    group_heads = index_heads // nk
    width = index_width // nk
    f32, bf16 = jnp.float32, jnp.bfloat16
    halves = 4
    dma = lambda *shape: pltpu.SemaphoreType.DMA(shape)
    in_vmem = pl.BlockSpec(memory_space=pltpu.VMEM)
    grad_query, grad_key, grad_weight = pl.pallas_call(
        kernel,
        in_specs=[pl.BlockSpec(memory_space=pl.ANY)] + [in_vmem] * 7,
        out_specs=[in_vmem] * 3,
        out_shape=[
            jax.ShapeDtypeStruct((rows, width), f32),
            jax.ShapeDtypeStruct((nh, keys_here // nh, dim), f32),
            jax.ShapeDtypeStruct((rows, group_heads), f32),
        ],
        scratch_shapes=[
            pltpu.VMEM((keys_here, lat), bf16),
            pltpu.VMEM((nk, rows, group_heads), f32),
            pltpu.VMEM((heads_here, keys_here, queries), f32),
            pltpu.VMEM((keys_here, queries), f32),
            pltpu.VMEM((keys_here, queries), f32),
            pltpu.VMEM((keys_here, queries), f32),
            pltpu.VMEM((lat, queries), bf16),
            pltpu.VMEM((lat, queries), bf16),
            pltpu.VMEM((2, 2, lat, queries), bf16),
            pltpu.VMEM((2, heads_here, queries), f32),
            pltpu.VMEM((nk - 1, 2, heads_here, queries), f32),
            pltpu.VMEM((heads_here, queries), f32),
            pltpu.VMEM((rows, keys_here), f32),
            pltpu.VMEM((rows, 128), f32),
            pltpu.VMEM((nk - 1, rows, 128), f32),
            pltpu.VMEM((halves, nh, rows, keys_here // halves), f32),
            pltpu.VMEM((nh - 1, halves, rows, keys_here // halves), f32),
            pltpu.VMEM((rows, keys_here), f32),
            pltpu.VMEM((dim, keys_here), f32),
            pltpu.VMEM((nh, keys_here // nh, dim), f32),
            pltpu.VMEM((nh - 1, keys_here // nh, dim), f32),
            pltpu.VMEM((nk, rows, width + 128), f32),
            pltpu.VMEM((nk - 1, rows, width + 128), f32),
            dma(4),
            dma(nk - 1), dma(nk - 1), dma(nk - 1), dma(nk - 1),
            dma(nh - 1, halves), dma(nh - 1, halves),
            dma(nk - 1), dma(nk - 1),
            dma(nh - 1), dma(nh - 1), dma(nh - 1), dma(nh - 1),
        ],
        compiler_params=pltpu.CompilerParams(
            collective_id=0, has_side_effects=True, vmem_limit_bytes=VMEM_LIMIT),
    )(q_latent.transpose(0, 2, 1), k_latent.T, key_start[None, :], query_pos[None, :], q_index, k_index,
      head_weight, loss_weight[None, :])
    return (grad_query, grad_key.reshape(keys_here, dim), grad_weight)


def solution(mesh):
    return jax.shard_map(
        shards,
        mesh=mesh,
        in_specs=(
            P("head", None, None),
            P("key", None),
            P("head", None),
            P("key", None),
            P("head", None),
            P("head"),
            P(),
            P(),
        ),
        out_specs=(P("head", "key"), P("key", None), P("head", "key")),
        check_vma=False,
    )
```
